128 devices in a mesh: scan: 32 (over z, y, core), col: 4 (over x).
Axes of the slice: x: 4, y: 4, z: 4, core: 2. Of those that a mesh axis runs over, the one named last changes fastest.
Arguments:
- raw_stack: bfloat16 [512, 2048, 512], P('scan', None, 'col'), may hold values from -10 to 10
- offsets: int32 [512], P('scan'), may hold values from 0 to 1788, as said below
Outputs:
- resampled: bfloat16 [512, 2048, 512], P('scan', None, 'col')
The draws below stay inside these ranges and needn't reach their ends.
Inputs may be any that keep to these rules, and one draw needn't show every extreme that they name: offsets[0] is 0 and every later entry exceeds the one before it by 3 or 4; by 4 in exactly (511) // 2 of these steps.
All inputs are finite; a program needn't handle non-finite values.
Results may differ from the reference program's by a relative error of at most 0.0056.
Values may be sent and summed in bfloat16 or wider, within the bound.
No kernel may reach another device: no remote copies, remote signals or barrier semaphores. Data moves between devices by JAX's collectives and lax.ppermute only.
A program may use at most 256 MiB of HBM per device.

```python
import jax
import jax.numpy as jnp
from jax import lax

ROWS = 2048
BAND = 512
PLANES = 512
SKEW = 1788


def draw_offsets(key, part):
    key = jax.random.fold_in(key, 7)
    step_count = PLANES - 1
    larger = step_count // 2
    increments = jnp.where(jnp.arange(step_count) < larger, 4, 3).astype(jnp.int32)
    shuffled = jax.random.permutation(key, increments)
    return jnp.concatenate([jnp.zeros((1,), jnp.int32), jnp.cumsum(shuffled).astype(jnp.int32)])


def levels(rng, dims, cuts, low, top_value):
    def one(axis_at, blocks):
        draws = jax.random.uniform(jax.random.fold_in(jax.random.fold_in(rng, 6), axis_at), (blocks,), jnp.float32, low / len(cuts), top_value / len(cuts))
        return jnp.repeat(jnp.exp(draws), dims[axis_at] // blocks).reshape((-1,) + (1,) * (len(dims) - axis_at - 1))

    gain = one(*cuts[0])
    for cut in cuts[1:]:
        gain = gain * one(*cut)
    return gain


def gaussian(own_key, extent, spread, bound, split=(), kind=jnp.bfloat16):
    values = jax.random.normal(own_key, extent, jnp.float32) * spread
    if len(split) > 0:
        values = levels(own_key, extent, split, -0.22, 0.18) * values
    return jnp.clip(values, min=-bound, max=bound).astype(kind)


def setup_inputs(seed: int = 0) -> dict:
    seeds = jax.random.split(jax.random.key(seed), 3)
    return {
        "raw_stack": gaussian(seeds[0], (PLANES, ROWS, BAND), 2.5, 10.0, ((0, 32), (2, 4))),
        "offsets": draw_offsets(jax.random.fold_in(seeds[2], 71), 0),
    }


EDGE = 0.25
MIDDLE = 0.5


def mix_padded(padded):
    planes_mixed = EDGE * padded[:-2] + MIDDLE * padded[1:-1] + EDGE * padded[2:]
    return EDGE * planes_mixed[:, :, :-2] + MIDDLE * planes_mixed[:, :, 1:-1] + EDGE * planes_mixed[:, :, 2:]


def shear_planes(values, row_start, plane_total, row_total):
    row_index = row_start + jnp.arange(values.shape[1], dtype=jnp.int32)
    numerator = (2 * row_index - row_total + 1) * plane_total
    whole_part = numerator // (4 * row_total)
    fraction = ((numerator - whole_part * (4 * row_total)).astype(jnp.float32) / (4.0 * row_total))[None, :, None]
    margin = plane_total // 4 + 2
    padded = jnp.pad(values, ((margin, margin), (0, 0), (0, 0)))

    def take_window(column, start):
        return lax.dynamic_slice_in_dim(column, (start + margin).astype(jnp.int32), plane_total + 1, 0)

    window = jax.vmap(take_window, in_axes=(1, 0), out_axes=1)(padded, whole_part)
    mixed = (1.0 - fraction) * window[:-1].astype(jnp.float32) + fraction * window[1:].astype(jnp.float32)
    return mixed.astype(jnp.bfloat16)


def shear_rows(values, plane_start, plane_total):
    plane_index = plane_start + jnp.arange(values.shape[0], dtype=jnp.int32)
    numerator = (2 * plane_index - plane_total + 1) * 17
    whole_part = numerator // 64
    fraction = ((numerator - whole_part * 64).astype(jnp.float32) / 64.0)[:, None, None]
    margin = 17 * plane_total // 64 + 2
    row_total = values.shape[1]
    padded = jnp.pad(values, ((0, 0), (margin, margin), (0, 0)))

    def take_window(single_plane, start):
        return lax.dynamic_slice_in_dim(single_plane, (start + margin).astype(jnp.int32), row_total + 1, 0)

    window = jax.vmap(take_window)(padded, whole_part)
    mixed = (1.0 - fraction) * window[:, :-1].astype(jnp.float32) + fraction * window[:, 1:].astype(jnp.float32)
    return mixed.astype(jnp.bfloat16)


def reference(raw_stack, offsets):
    def deskew_plane(inputs):
        single_plane, shift_rows = inputs
        padded = jnp.pad(single_plane, ((ROWS, ROWS), (0, 0)))
        return lax.dynamic_slice_in_dim(padded, (ROWS - shift_rows + SKEW // 2).astype(jnp.int32), ROWS, 0)

    deskewed = lax.map(deskew_plane, (raw_stack, offsets))
    padded = jnp.pad(deskewed.astype(jnp.float32), ((1, 1), (0, 0), (1, 1)))
    smoothed = mix_padded(padded).astype(jnp.bfloat16)
    block_count = BAND // 128
    blocks = smoothed.reshape(PLANES, ROWS, block_count, 128).transpose(2, 0, 1, 3)

    def column_block(block):
        return shear_rows(shear_planes(block, 0, PLANES, ROWS), 0, PLANES)

    result = lax.map(column_block, blocks)
    return result.transpose(1, 2, 0, 3).reshape(PLANES, ROWS, BAND)
```

```python
import functools

import jax
import jax.numpy as jnp
from jax import lax
from jax.experimental import pallas as pl
from jax.experimental.pallas import tpu as pltpu
from jax.sharding import PartitionSpec as P

SLAB = 16
ROWS = 2048
COLS = 128
BLOCK = 128
PARTS = ROWS // BLOCK
SENDS = PARTS + 1
HALF_SKEW = 894
SCANS = 32
HELD = SLAB + 3
PAD = 128
EDGE_ROWS = 512
MARGIN = 144
VMEM_LIMIT = 60 * 1024 * 1024

ORDER = (4, -4, 8, -8, 3, -3, 7, -7, 5, -5, 1, -1, 2, -2, 6, -6)


def dot(a, b):
    return jnp.dot(a, b, preferred_element_type=jnp.float32)


def pack_edges_kernel(raw_ref, out_ref, planes, sem):
    def fetch(p):
        return pltpu.make_async_copy(raw_ref.at[p], planes.at[p], sem.at[p])

    for p in range(SLAB):
        fetch(p).start()
    src = lax.broadcasted_iota(jnp.int32, (COLS, COLS), 0)
    dst = lax.broadcasted_iota(jnp.int32, (COLS, COLS), 1)
    acc = [jnp.zeros((EDGE_ROWS, COLS), jnp.float32)]

    def one(p, total):
        fetch(p).wait()
        for g in range(4):
            pick = ((src == COLS - 1) & (dst == 32 * g + p)) | ((src == 0) & (dst == 32 * g + 16 + p))
            pick = jnp.where(pick, 1.0, 0.0).astype(jnp.bfloat16)
            total = total + dot(planes[p, EDGE_ROWS * g : EDGE_ROWS * (g + 1), :], pick)
        return total

    out_ref[...] = lax.fori_loop(0, SLAB, one, acc[0]).astype(jnp.bfloat16)


def pack_edges(raw):
    return pl.pallas_call(
        pack_edges_kernel,
        out_shape=jax.ShapeDtypeStruct((EDGE_ROWS, COLS), jnp.bfloat16),
        in_specs=[pl.BlockSpec(memory_space=pl.ANY)],
        out_specs=pl.BlockSpec(memory_space=pltpu.VMEM),
        scratch_shapes=[
            pltpu.VMEM((SLAB, ROWS, COLS), jnp.bfloat16),
            pltpu.SemaphoreType.DMA((SLAB,)),
        ],
        compiler_params=pltpu.CompilerParams(vmem_limit_bytes=VMEM_LIMIT),
        cost_estimate=pl.CostEstimate(flops=2 * SLAB * ROWS * COLS * COLS, bytes_accessed=2 * SLAB * ROWS * COLS, transcendentals=0),
        name="pack_edges",
    )(raw)


def shear_kernel(meta, raw_ref, before_ref, after_ref, edge_ref, edge_before, edge_after, *rest):
    outs = rest[:SENDS]
    planes, held, packed, sem, out_sem = rest[SENDS:]
    device = meta[HELD]

    def fetch_own():
        return pltpu.make_async_copy(raw_ref, planes.at[pl.ds(1, SLAB)], sem.at[0])

    def fetch_before():
        return pltpu.make_async_copy(before_ref, planes.at[pl.ds(0, 1)], sem.at[1])

    def fetch_after():
        return pltpu.make_async_copy(after_ref, planes.at[pl.ds(SLAB + 1, 2)], sem.at[2])

    for f in (fetch_own, fetch_before, fetch_after):
        f().start()

    zeros = jnp.zeros((PAD, COLS), jnp.float32)

    def clear(p, _):
        held[p, 0:PAD, :] = zeros
        held[p, PAD + ROWS : PAD + ROWS + PAD, :] = zeros
        return 0

    lax.fori_loop(0, HELD, clear, 0)
    for f in (fetch_own, fetch_before, fetch_after):
        f().wait()

    src = lax.broadcasted_iota(jnp.int32, (COLS, COLS), 0)
    dst = lax.broadcasted_iota(jnp.int32, (COLS, COLS), 1)
    tri = jnp.where(src == dst, 0.125, jnp.where(jnp.abs(src - dst) == 1, 0.0625, 0.0)).astype(jnp.bfloat16)

    def smooth(slot, plane, edges):
        for g in range(4):
            hit = ((src == 32 * g + plane) & (dst == 0)) | ((src == 32 * g + 16 + plane) & (dst == COLS - 1))
            edge = jnp.where(hit, 0.0625, 0.0).astype(jnp.bfloat16)
            weights = jnp.concatenate([tri, edge], axis=0)
            values = jnp.concatenate([planes[slot, EDGE_ROWS * g : EDGE_ROWS * (g + 1), :], edges[...]], axis=1)
            held[slot, PAD + EDGE_ROWS * g : PAD + EDGE_ROWS * (g + 1), :] = dot(values, weights)

    smooth(0, SLAB - 1, edge_before)

    def own(p, _):
        smooth(p + 1, p, edge_ref)
        return 0

    lax.fori_loop(0, SLAB, own, 0)
    smooth(SLAB + 1, 0, edge_after)
    smooth(SLAB + 2, 1, edge_after)

    share = (2 * lax.broadcasted_iota(jnp.int32, (8, COLS), 0) + 1).astype(jnp.float32) * 0.0625
    last = device == SCANS - 1

    def send(b, _):
        low = b < SENDS // 2
        role = jnp.logical_and(last, low)
        end = jnp.logical_and(last, jnp.logical_not(low))
        keep_15 = jnp.where(role, 0.0, 1.0).astype(jnp.float32)
        keep_16 = jnp.where(end, 0.0, 1.0).astype(jnp.float32)

        def starts(block, none):
            found = []
            for slot in range(HELD):
                dead = jnp.logical_or(none, role if slot <= SLAB else end)
                start = PAD + HALF_SKEW + block * BLOCK - meta[slot]
                start = jnp.clip(start, 0, PAD + ROWS)
                found.append(jnp.where(dead, 0, start))
            return found

        here = starts(b, b == SENDS - 1)
        above = starts(b - 1, b == 0)

        def mixed(r, bases, first, stop):
            x = {p: held[p + 1, pl.ds(bases[p + 1] + 8 * r, 8), :] for p in range(first - 1, stop + 2)}
            u = {}
            for p in range(first, stop + 1):
                u[p] = x[p - 1] + x[p + 1] + (x[p] + x[p])
                if p == SLAB - 1:
                    u[p] = u[p] * keep_15
                if p == SLAB:
                    u[p] = u[p] * keep_16
            return {p: u[p] + share * (u[p + 1] - u[p]) for p in range(first, stop)}

        def both(r):
            got = dict(mixed(r, here, r, SLAB))
            if r:
                got.update({p + SLAB: v for p, v in mixed(r, above, 0, r).items()})
            return got

        for t in range(8):
            even, odd = both(2 * t), both(2 * t + 1)
            for q in range(SLAB):
                tile = jnp.concatenate([even[q + 2 * t], odd[q + 2 * t + 1]], axis=0)
                packed[b, q, 16 * t : 16 * t + 16, :] = tile.astype(jnp.bfloat16)
        for i in range(SENDS):

            @pl.when(b == i)
            def _():
                pltpu.make_async_copy(packed.at[i], outs[i], out_sem.at[i]).start()

        return 0

    lax.fori_loop(0, SENDS, send, 0)
    for i in range(SENDS):
        pltpu.make_async_copy(packed.at[i], outs[i], out_sem.at[i]).wait()


def shear(meta, raw, before, after, edges, edges_before, edges_after):
    part = jax.ShapeDtypeStruct((SLAB, BLOCK, COLS), jnp.bfloat16)
    hbm = pl.BlockSpec(memory_space=pl.ANY)
    vmem = pl.BlockSpec(memory_space=pltpu.VMEM)
    return pl.pallas_call(
        shear_kernel,
        out_shape=(part,) * SENDS,
        in_specs=[pl.BlockSpec(memory_space=pltpu.SMEM), hbm, hbm, hbm, vmem, vmem, vmem],
        out_specs=(hbm,) * SENDS,
        scratch_shapes=[
            pltpu.VMEM((HELD, ROWS, COLS), jnp.bfloat16),
            pltpu.VMEM((HELD, PAD + ROWS + PAD, COLS), jnp.float32),
            pltpu.VMEM((SENDS, SLAB, BLOCK, COLS), jnp.bfloat16),
            pltpu.SemaphoreType.DMA((3,)),
            pltpu.SemaphoreType.DMA((SENDS,)),
        ],
        compiler_params=pltpu.CompilerParams(vmem_limit_bytes=VMEM_LIMIT),
        name="shear_planes",
    )(meta, raw, before, after, edges, edges_before, edges_after)


def rows_kernel(meta, *rest):
    parts = [None] * SENDS
    for at, c in enumerate(ORDER + (0,)):
        parts[c + 8] = rest[at]
    out_ref, got, full, done, sem, out_sem = rest[SENDS:]
    device = meta[HELD]

    def fetch(i):
        return pltpu.make_async_copy(parts[i], got.at[i], sem.at[i])

    for i in range(SENDS):
        fetch(i).start()
    zeros = jnp.zeros((MARGIN, COLS), jnp.float32)

    def clear(q, _):
        full[q, 0:MARGIN, :] = zeros
        full[q, MARGIN + ROWS : MARGIN + ROWS + MARGIN, :] = zeros
        return 0

    lax.fori_loop(0, SLAB, clear, 0)
    for i in range(SENDS):
        fetch(i).wait()
    upper = lax.broadcasted_iota(jnp.int32, (16, COLS), 0) < 8

    def merge(b, _):
        for q in range(SLAB):
            for t in range(8):
                rows = slice(16 * t, 16 * t + 16)
                if q + 2 * t + 1 < SLAB:
                    tile = got[b, q, rows, :].astype(jnp.float32)
                elif q + 2 * t >= SLAB:
                    tile = got[b + 1, q, rows, :].astype(jnp.float32)
                else:
                    tile = jnp.where(upper, got[b, q, rows, :].astype(jnp.float32), got[b + 1, q, rows, :].astype(jnp.float32))
                full[q, pl.ds(pl.multiple_of(MARGIN + b * BLOCK + 16 * t, 16), 16), :] = tile
        return 0

    lax.fori_loop(0, PARTS, merge, 0)

    def put(q):
        return pltpu.make_async_copy(done.at[q], out_ref.at[q], out_sem.at[q])

    def plane(q, _):
        numerator = 17 * (2 * (device * SLAB + q) - (SLAB * SCANS - 1))
        start = MARGIN + lax.shift_right_arithmetic(numerator, 6)
        share = (numerator & 63).astype(jnp.float32) * (1.0 / 64.0)

        def rows(i, _):
            for t in range(16):
                base = start + i * 256 + 16 * t
                a = full[q, pl.ds(base, 16), :]
                c = full[q, pl.ds(base + 1, 16), :]
                done[q, pl.ds(pl.multiple_of(i * 256 + 16 * t, 16), 16), :] = (a + share * (c - a)).astype(jnp.bfloat16)
            return 0

        lax.fori_loop(0, ROWS // 256, rows, 0)
        put(q).start()
        return 0

    lax.fori_loop(0, SLAB, plane, 0)
    for q in range(SLAB):
        put(q).wait()


def shear_rows(meta, parts):
    hbm = pl.BlockSpec(memory_space=pl.ANY)
    return pl.pallas_call(
        rows_kernel,
        out_shape=jax.ShapeDtypeStruct((SLAB, ROWS, COLS), jnp.bfloat16),
        in_specs=[pl.BlockSpec(memory_space=pltpu.SMEM)] + [hbm] * SENDS,
        out_specs=hbm,
        scratch_shapes=[
            pltpu.VMEM((SENDS, SLAB, BLOCK, COLS), jnp.bfloat16),
            pltpu.VMEM((SLAB, MARGIN + ROWS + MARGIN, COLS), jnp.float32),
            pltpu.VMEM((SLAB, ROWS, COLS), jnp.bfloat16),
            pltpu.SemaphoreType.DMA((SENDS,)),
            pltpu.SemaphoreType.DMA((SLAB,)),
        ],
        compiler_params=pltpu.CompilerParams(vmem_limit_bytes=VMEM_LIMIT),
        name="shear_rows",
    )(meta, *parts)


def pairs_of(c):
    found = [(s, s - c) for s in range(SCANS) if 0 <= s - c < SCANS]
    if c < 0:
        found.append((SCANS - 1, -c - 1))
    return found


def local(raw, offsets):
    device = lax.axis_index("scan")
    up = [(i, i + 1) for i in range(SCANS - 1)]
    down = [((i + 1) % SCANS, i) for i in range(SCANS)]
    right = [(i, i + 1) for i in range(3)]
    left = [(i + 1, i) for i in range(3)]
    after = lax.ppermute(raw[:2], "scan", down)
    before = lax.ppermute(raw[SLAB - 1 :], "scan", up)
    offsets_after = lax.ppermute(offsets[:2], "scan", down)
    offsets_before = lax.ppermute(offsets[SLAB - 1 :], "scan", up)
    own = pack_edges(raw)
    from_left = lax.ppermute(own, "col", right)
    from_right = lax.ppermute(own, "col", left)
    lane = lax.broadcasted_iota(jnp.int32, own.shape, 1)
    edges = jnp.where(lane % 32 < 16, from_left, from_right)
    edges_after = lax.ppermute(edges, "scan", down)
    edges_before = lax.ppermute(edges, "scan", up)
    meta = jnp.concatenate([offsets_before, offsets, offsets_after, device[None].astype(jnp.int32)])
    parts = list(shear(meta, raw, before, after, edges, edges_before, edges_after))
    moved = [lax.ppermute(parts[c + 8], "scan", pairs_of(c)) for c in ORDER]
    return shear_rows(meta, moved + [parts[8]])


def solution(mesh):
    placed = (P("scan", None, "col"), P("scan"))
    return jax.shard_map(local, mesh=mesh, in_specs=placed, out_specs=P("scan", None, "col"), check_vma=False)
```

```python
import functools

import jax
import jax.numpy as jnp
import numpy as np
from jax import lax
from jax.experimental import pallas as pl
from jax.experimental.pallas import tpu as pltpu
from jax.sharding import PartitionSpec as P

SLAB = 16
ROWS = 2048
COLS = 128
BLOCK = 128
SENDS = ROWS // BLOCK + 1
HALF_SKEW = 894
SCANS = 32
HELD = SLAB + 3
PAD = 128
EDGE_ROWS = 512
MARGIN = 144
VMEM_LIMIT = 60 * 1024 * 1024

ORDER = (4, -4, 8, -8, 3, -3, 7, -7, 5, -5, 1, -1, 2, -2, 6, -6)
EARLY = ORDER[:8]
LATE = ORDER[8:] + (0,)
CODED = ROWS + 16
FIRST, STOP = 3, 13

HBM = pl.BlockSpec(memory_space=pl.ANY)
VMEM = pl.BlockSpec(memory_space=pltpu.VMEM)
SMEM = pl.BlockSpec(memory_space=pltpu.SMEM)

COST = pl.CostEstimate(flops=1000, bytes_accessed=1000, transcendentals=0)


def dot(a, b):
    return jnp.dot(a, b, preferred_element_type=jnp.float32)


def halos_kernel(offsets, raw_ref, first_ref, final_ref, planes, sem, out_sem):
    sides = ((first_ref, 0, 0), (first_ref, 1, 1), (final_ref, 0, SLAB - 1))
    loads = [pltpu.make_async_copy(raw_ref.at[p], planes.at[n, pl.ds(0, ROWS)], sem.at[n]) for n, (_, _, p) in enumerate(sides)]
    for load in loads:
        load.start()
    lane = lax.broadcasted_iota(jnp.int32, (16, COLS), 1)
    for n, (_, _, p) in enumerate(sides):
        shift = offsets[p]
        code = jnp.where(lane == 0, lax.shift_right_logical(shift, 4), jnp.where(lane == 1, shift & 15, 0))
        planes[n, ROWS:CODED, :] = code.astype(jnp.float32).astype(jnp.bfloat16)
    stores = []
    for n, (ref, at, _) in enumerate(sides):
        loads[n].wait()
        stores.append(pltpu.make_async_copy(planes.at[n], ref.at[at], out_sem.at[n]))
        stores[-1].start()
    for store in stores:
        store.wait()


def halos(offsets, raw):
    return pl.pallas_call(
        halos_kernel,
        out_shape=tuple(jax.ShapeDtypeStruct((n, CODED, COLS), jnp.bfloat16) for n in (2, 1)),
        in_specs=[SMEM, HBM],
        out_specs=(HBM, HBM),
        scratch_shapes=[pltpu.VMEM((3, CODED, COLS), jnp.bfloat16), pltpu.SemaphoreType.DMA((3,)), pltpu.SemaphoreType.DMA((3,))],
        cost_estimate=COST,
        name="halos",
    )(offsets, raw)


def pack_edges_kernel(raw_ref, out_ref, planes, sem):
    def fetch(g):
        rows = pl.ds(EDGE_ROWS * g, EDGE_ROWS)
        return pltpu.make_async_copy(raw_ref.at[:, rows], planes.at[:, rows], sem.at[g])

    for g in range(4):
        fetch(g).start()
    src = lax.broadcasted_iota(jnp.int32, (SLAB * COLS, COLS), 0)
    dst = lax.broadcasted_iota(jnp.int32, (SLAB * COLS, COLS), 1)
    pick = (src == COLS * dst + COLS - 1) | (src == COLS * (dst - 16))
    pick = jnp.where(pick & (dst < 32), 1.0, 0.0).astype(jnp.bfloat16)
    total = None
    for g in range(4):
        fetch(g).wait()
        rows = slice(EDGE_ROWS * g, EDGE_ROWS * (g + 1))
        values = jnp.concatenate([planes[p, rows, :] for p in range(SLAB)], axis=1)
        found = dot(values, pick)
        total = found if g == 0 else total + pltpu.roll(found, 32 * g, 1)
    out_ref[...] = total.astype(jnp.bfloat16)


def pack_edges(raw):
    return pl.pallas_call(
        pack_edges_kernel,
        out_shape=jax.ShapeDtypeStruct((EDGE_ROWS, COLS), jnp.bfloat16),
        in_specs=[HBM],
        out_specs=VMEM,
        scratch_shapes=[
            pltpu.VMEM((SLAB, ROWS, COLS), jnp.bfloat16),
            pltpu.SemaphoreType.DMA((4,)),
        ],
        compiler_params=pltpu.CompilerParams(vmem_limit_bytes=VMEM_LIMIT),
        cost_estimate=COST,
        name="pack_edges",
    )(raw)


def column_weights():
    held = np.zeros((SLAB, 2 * COLS, COLS), np.float32)
    for at in range(COLS):
        held[:, at, at] = 0.125
        held[:, at, [n for n in (at - 1, at + 1) if 0 <= n < COLS]] = 0.0625
    for p in range(SLAB):
        for g in range(4):
            held[p, COLS + 32 * g + p, 0] = 0.0625
            held[p, COLS + 32 * g + 16 + p, COLS - 1] = 0.0625
    return jnp.asarray(held, jnp.bfloat16)


def shear_kernel(group, offsets, raw_ref, before_ref, after_ref, *rest):
    count = len(group)
    late = group == LATE
    if late:
        weights_ref, edges_before, edges_own, edges_after, *rest = rest
    outs, rest = rest[:count], rest[count:]
    planes, held, packed, codes, offs, sem, out_sem, code_sem, *rest = rest
    device = lax.axis_index("scan")
    last = device == SCANS - 1
    beside_refs = ((0, before_ref, 0), (SLAB + 1, after_ref, 0), (SLAB + 2, after_ref, 1))

    code_copies = [
        pltpu.make_async_copy(ref.at[p, pl.ds(ROWS, 16)], codes.at[n], code_sem.at[n])
        for n, (_, ref, p) in enumerate(beside_refs)
    ]
    loads = []
    for slot in range(HELD):
        ref, p = (before_ref, 0) if slot == 0 else (raw_ref, slot - 1) if slot <= SLAB else (after_ref, slot - SLAB - 1)
        loads.append(pltpu.make_async_copy(ref.at[p, pl.ds(0, ROWS)], planes.at[slot], sem.at[slot]))
    for load in loads + code_copies:
        load.start()
    for p in range(SLAB):
        offs[p + 1] = offsets[p]
    zeros = jnp.zeros((PAD, COLS), jnp.float32)
    for slot in range(HELD):
        held[slot, 0:PAD, :] = zeros
        held[slot, PAD + ROWS : PAD + ROWS + PAD, :] = zeros
    if late:
        beside, weights, weights_sem = rest
        weights_copy = pltpu.make_async_copy(weights_ref, weights, weights_sem)
        weights_copy.start()
        lane = lax.broadcasted_iota(jnp.int32, (EDGE_ROWS, COLS), 1)
        for e, edges in enumerate((edges_before, edges_own, edges_after)):
            values = edges[...].astype(jnp.float32)
            for g in range(4):
                mine = (lane >= 32 * g) & (lane < 32 * g + 32)
                beside[e, EDGE_ROWS * g : EDGE_ROWS * (g + 1), :] = jnp.where(mine, values, 0.0).astype(jnp.bfloat16)
        weights_copy.wait()
    for slot in range(HELD):
        loads[slot].wait()
        if late:
            e = 0 if slot == 0 else 1 if slot <= SLAB else 2
            values = jnp.concatenate([planes[slot], beside[e]], axis=1)
            held[slot, PAD : PAD + ROWS, :] = dot(values, weights[(slot + SLAB - 1) % SLAB])
        else:
            held[slot, PAD : PAD + ROWS, :] = planes[slot].astype(jnp.float32) * 0.25
    row = lax.broadcasted_iota(jnp.int32, (16, COLS), 0)
    lane = lax.broadcasted_iota(jnp.int32, (16, COLS), 1)
    scale = jnp.where(row == 0, jnp.where(lane == 0, 16.0, jnp.where(lane == 1, 1.0, 0.0)), 0.0)
    for n, (slot, _, _) in enumerate(beside_refs):
        code_copies[n].wait()
        offs[slot] = jnp.sum(codes[n].astype(jnp.float32) * scale).astype(jnp.int32)

    def block_of(i):
        found = jnp.int32(group[0] + 8)
        for at, c in enumerate(group[1:]):
            found = jnp.where(i == at + 1, c + 8, found)
        return found

    share = (2 * lax.broadcasted_iota(jnp.int32, (8, COLS), 0) + 1).astype(jnp.float32) * 0.0625

    def send(i, _):
        b = block_of(i)
        low = b < SENDS // 2
        role = jnp.logical_and(last, low)
        end = jnp.logical_and(last, jnp.logical_not(low))
        keep_15 = jnp.where(role, 0.0, 1.0).astype(jnp.float32)
        keep_16 = jnp.where(end, 0.0, 1.0).astype(jnp.float32)

        def starts(block, none):
            found = []
            for slot in range(HELD):
                dead = jnp.logical_or(none, role if slot <= SLAB else end)
                start = jnp.clip(PAD + HALF_SKEW + block * BLOCK - offs[slot], 0, PAD + ROWS)
                found.append(jnp.where(dead, 0, start))
            return found

        here = starts(b, b == SENDS - 1)
        above = starts(b - 1, b == 0)

        def mixed(r, bases, first, stop):
            x = {p: held[p + 1, pl.ds(bases[p + 1] + 8 * r, 8), :] for p in range(first - 1, stop + 2)}
            v = {p: x[p] + x[p + 1] for p in range(first - 1, stop + 1)}
            u = {}
            for p in range(first, stop + 1):
                u[p] = v[p - 1] + v[p]
                if p == SLAB - 1:
                    u[p] = u[p] * keep_15
                if p == SLAB:
                    u[p] = u[p] * keep_16
            return {p: u[p] + share * (u[p + 1] - u[p]) for p in range(first, stop)}

        def both(r):
            got = dict(mixed(r, here, r, SLAB))
            if r:
                got.update({p + SLAB: v for p, v in mixed(r, above, 0, r).items()})
            got = [got[q + r] for q in range(SLAB)]
            return got

        for t in range(8):
            even, odd = both(2 * t), both(2 * t + 1)
            for q in range(SLAB):
                tile = jnp.concatenate([even[q], odd[q]], axis=0)
                packed[i, q, 16 * t : 16 * t + 16, :] = tile.astype(jnp.bfloat16)
        for at in range(count):

            @pl.when(i == at)
            def _():
                pltpu.make_async_copy(packed.at[at], outs[at], out_sem.at[at]).start()

        return 0

    lax.fori_loop(0, count, send, 0)
    for at in range(count):
        pltpu.make_async_copy(packed.at[at], outs[at], out_sem.at[at]).wait()


PART = jax.ShapeDtypeStruct((SLAB, BLOCK, COLS), jnp.bfloat16)


def shear(group, *operands):
    count = len(group)
    late = group == LATE
    extra = [
        pltpu.VMEM((3, ROWS, COLS), jnp.bfloat16),
        pltpu.VMEM((SLAB, 2 * COLS, COLS), jnp.bfloat16),
        pltpu.SemaphoreType.DMA,
    ]
    return pl.pallas_call(
        functools.partial(shear_kernel, group),
        out_shape=(PART,) * count,
        in_specs=[SMEM, HBM, HBM, HBM] + ([HBM, VMEM, VMEM, VMEM] if late else []),
        out_specs=(HBM,) * count,
        scratch_shapes=[
            pltpu.VMEM((HELD, ROWS, COLS), jnp.bfloat16),
            pltpu.VMEM((HELD, PAD + ROWS + PAD, COLS), jnp.float32),
            pltpu.VMEM((count, SLAB, BLOCK, COLS), jnp.bfloat16),
            pltpu.VMEM((3, 16, COLS), jnp.bfloat16),
            pltpu.SMEM((HELD,), jnp.int32),
            pltpu.SemaphoreType.DMA((HELD,)),
            pltpu.SemaphoreType.DMA((count,)),
            pltpu.SemaphoreType.DMA((3,)),
        ]
        + (extra if late else []),
        compiler_params=pltpu.CompilerParams(vmem_limit_bytes=VMEM_LIMIT),
        cost_estimate=COST,
        name="shear_planes",
    )(*operands)


def pack_parts_kernel(*refs):
    parts, out_ref = refs[:-1], refs[-1]
    pair = lax.shift_right_logical(lax.broadcasted_iota(jnp.int32, (16, COLS), 1), 1)
    for first in range(0, len(parts), 4):
        for t in range(8):
            rows = slice(16 * t, 16 * t + 16)
            total = jnp.zeros((16, COLS), jnp.float32)
            for n, part in enumerate(parts[first : first + 4]):
                for q in range(SLAB):
                    found = pltpu.roll(part[q, rows, :].astype(jnp.float32), (32 * n + 2 * q + 1) % COLS, 1)
                    total = jnp.where(pair == 16 * n + q, found, total)
            out_ref[32 * first + 16 * t : 32 * first + 16 * t + 16, :] = total.astype(jnp.bfloat16)


def pack_parts(*parts):
    return pl.pallas_call(
        pack_parts_kernel,
        out_shape=jax.ShapeDtypeStruct((BLOCK * len(parts) // 4, COLS), jnp.bfloat16),
        in_specs=[VMEM] * len(parts),
        out_specs=VMEM,
        compiler_params=pltpu.CompilerParams(vmem_limit_bytes=VMEM_LIMIT),
        cost_estimate=COST,
        name="pack_parts",
    )(*parts)


def smooth_parts_kernel(from_left, from_right, *refs):
    count = len(refs) // 2
    parts, outs = refs[:count], refs[count:]
    src = lax.broadcasted_iota(jnp.int32, (COLS, COLS), 0)
    dst = lax.broadcasted_iota(jnp.int32, (COLS, COLS), 1)
    tri = jnp.where(src == dst, 0.5, jnp.where(jnp.abs(src - dst) == 1, 0.25, 0.0)).astype(jnp.bfloat16)
    left_lane = (lax.broadcasted_iota(jnp.int32, from_left.shape, 1) & 1) == 0
    edges = jnp.where(left_lane, from_left[...].astype(jnp.float32), from_right[...].astype(jnp.float32)).astype(jnp.bfloat16)
    for n in range(count):
        for q in range(SLAB):
            lane = 32 * (n % 4) + 2 * q
            hit = ((src == lane) & (dst == 0)) | ((src == lane + 1) & (dst == COLS - 1))
            weights = jnp.concatenate([tri, jnp.where(hit, 0.25, 0.0).astype(jnp.bfloat16)], axis=0)
            values = jnp.concatenate([parts[n][q], edges[BLOCK * (n // 4) : BLOCK * (n // 4 + 1)]], axis=1)
            outs[n][q] = dot(values, weights).astype(jnp.bfloat16)


def smooth_parts(from_left, from_right, *parts):
    return pl.pallas_call(
        smooth_parts_kernel,
        out_shape=(jax.ShapeDtypeStruct((SLAB, BLOCK, COLS), jnp.bfloat16),) * len(parts),
        in_specs=[VMEM] * (2 + len(parts)),
        out_specs=(VMEM,) * len(parts),
        compiler_params=pltpu.CompilerParams(vmem_limit_bytes=VMEM_LIMIT),
        cost_estimate=COST,
        name="smooth_parts",
    )(from_left, from_right, *parts)


def merge(got, full, at, blocks, top):
    upper = lax.broadcasted_iota(jnp.int32, (16, COLS), 0) < 8

    def one(b, _):
        for q in range(SLAB):
            for t in range(8):
                rows = slice(16 * t, 16 * t + 16)
                if q + 2 * t + 1 < SLAB:
                    tile = got[at + b, q, rows, :].astype(jnp.float32)
                elif q + 2 * t >= SLAB:
                    tile = got[at + b + 1, q, rows, :].astype(jnp.float32)
                else:
                    ours = got[at + b, q, rows, :].astype(jnp.float32)
                    tile = jnp.where(upper, ours, got[at + b + 1, q, rows, :].astype(jnp.float32))
                full[q, pl.ds(pl.multiple_of(top + b * BLOCK + 16 * t, 16), 16), :] = tile
        return 0

    lax.fori_loop(0, blocks, one, 0)


def shift_of(q):
    numerator = 17 * (2 * (lax.axis_index("scan") * SLAB + q) - (SLAB * SCANS - 1))
    whole = lax.shift_right_arithmetic(numerator, 6)
    share = (numerator & 63).astype(jnp.float32) * (1.0 / 64.0)
    tile = -lax.shift_right_arithmetic(whole, 4)
    return whole, share, tile


def interpolate(full, done, q, source, target, tiles, share):
    for t in range(tiles):
        a = full[q, pl.ds(source + 16 * t, 16), :]
        c = full[q, pl.ds(source + 1 + 16 * t, 16), :]
        done[q, pl.ds(pl.multiple_of(target + 16 * t, 16), 16), :] = (a + share * (c - a)).astype(jnp.bfloat16)


INNER = (STOP - FIRST) * BLOCK - 16
OUTER = 272
LOW = FIRST * BLOCK
HIGH = LOW + INNER


def inner_kernel(*refs):
    count = STOP - FIRST + 1
    parts = refs[:count]
    out_ref, got, full, done, sem, out_sem = refs[count:]

    def fetch(i):
        return pltpu.make_async_copy(parts[i], got.at[i], sem.at[i])

    for i in range(count):
        fetch(i).start()
    for i in range(count):
        fetch(i).wait()
    merge(got, full, 0, STOP - FIRST, 0)

    def put(q, tile):
        return pltpu.make_async_copy(done.at[q], out_ref.at[q, pl.ds(pl.multiple_of(LOW + 16 * tile, 16), INNER)], out_sem.at[q])

    def plane(q, _):
        whole, share, tile = shift_of(q)
        interpolate(full, done, q, 16 * tile + whole, 0, INNER // 16, share)
        put(q, tile).start()
        return 0

    lax.fori_loop(0, SLAB, plane, 0)
    for q in range(SLAB):
        put(q, shift_of(q)[2]).wait()


def outer_kernel(*refs):
    top, bottom = FIRST + 2, SENDS - STOP + 1
    count = top + bottom
    parts = refs[:count]
    _, out_ref, got, full, done, sem, out_sem = refs[count:]

    def fetch(i):
        return pltpu.make_async_copy(parts[i], got.at[i], sem.at[i])

    for i in range(count):
        fetch(i).start()
    zeros = jnp.zeros((MARGIN, COLS), jnp.float32)
    low_rows, high_rows = (top - 1) * BLOCK, (bottom - 1) * BLOCK
    base = MARGIN + low_rows
    first_row = ROWS - high_rows

    def clear(q, _):
        full[q, 0:MARGIN, :] = zeros
        full[q, base + high_rows : base + high_rows + MARGIN, :] = zeros
        return 0

    lax.fori_loop(0, SLAB, clear, 0)
    for i in range(count):
        fetch(i).wait()
    merge(got, full, 0, top - 1, MARGIN)
    merge(got, full, top, bottom - 1, base)

    def targets(tile):
        low = jnp.maximum(LOW + 16 * tile - OUTER, 0)
        high = jnp.minimum(HIGH + 16 * tile, ROWS - OUTER)
        return 0, low, high, ROWS - OUTER

    def puts(q, tile):
        return [
            pltpu.make_async_copy(
                done.at[q, pl.ds(OUTER * n, OUTER)], out_ref.at[q, pl.ds(pl.multiple_of(row, 16), OUTER)], out_sem.at[q, n]
            )
            for n, row in enumerate(targets(tile))
        ]

    def plane(q, _):
        whole, share, tile = shift_of(q)
        for n, row in enumerate(targets(tile)):
            source = row + whole + (MARGIN if n < 2 else base - first_row)
            interpolate(full, done, q, source, OUTER * n, OUTER // 16, share)
        for put in puts(q, tile)[::3]:
            put.start()

        @pl.when(q >= 2)
        def _():
            inward(q - 2)

        return 0

    def inward(q):
        first, low, high, final = puts(q, shift_of(q)[2])
        first.wait()
        final.wait()
        low.start()
        high.start()

    lax.fori_loop(0, SLAB, plane, 0)
    for q in range(SLAB - 2, SLAB):
        inward(q)
    for q in range(SLAB):
        for put in puts(q, shift_of(q)[2])[1:3]:
            put.wait()


def row_shear(kernel, parts, rows, full_rows, puts, into=None):
    count = len(parts)
    operands = list(parts) + ([] if into is None else [into])
    return pl.pallas_call(
        kernel,
        out_shape=jax.ShapeDtypeStruct((SLAB, ROWS, COLS), jnp.bfloat16),
        in_specs=[HBM] * len(operands),
        out_specs=HBM,
        scratch_shapes=[
            pltpu.VMEM((count, SLAB, BLOCK, COLS), jnp.bfloat16),
            pltpu.VMEM((SLAB, full_rows, COLS), jnp.float32),
            pltpu.VMEM((SLAB, rows, COLS), jnp.bfloat16),
            pltpu.SemaphoreType.DMA((count,)),
            pltpu.SemaphoreType.DMA((SLAB,) + puts),
        ],
        input_output_aliases={} if into is None else {count: 0},
        compiler_params=pltpu.CompilerParams(vmem_limit_bytes=VMEM_LIMIT),
        cost_estimate=COST,
        name="shear_rows",
    )(*operands)


def pairs_of(c):
    found = [(s, s - c) for s in range(SCANS) if 0 <= s - c < SCANS]
    if c < 0:
        found.append((SCANS - 1, -c - 1))
    return found


def local(raw, offsets):
    up = [(i, i + 1) for i in range(SCANS - 1)]
    down = [((i + 1) % SCANS, i) for i in range(SCANS)]
    right = [(i, i + 1) for i in range(3)]
    left = [(i + 1, i) for i in range(3)]
    first, final = halos(offsets, raw)
    after = lax.ppermute(first, "scan", down)
    before = lax.ppermute(final, "scan", up)
    own = pack_edges(raw)
    from_left = lax.ppermute(own, "col", right)
    from_right = lax.ppermute(own, "col", left)
    raw, _ = lax.optimization_barrier((raw, own))
    made = shear(EARLY, offsets, raw, before, after)
    moved = {c: lax.ppermute(part, "scan", pairs_of(c)) for c, part in zip(EARLY, made)}
    lane = lax.broadcasted_iota(jnp.int32, own.shape, 1)
    edges = jnp.where(lane % 32 < 16, from_left, from_right)
    edges, _ = lax.optimization_barrier((edges, made[0]))
    edges_after = lax.ppermute(edges, "scan", down)
    edges_before = lax.ppermute(edges, "scan", up)
    made = shear(LATE, offsets, raw, before, after, column_weights(), edges_before, edges, edges_after)
    parts = dict(zip(LATE, made))
    for c in ORDER[len(EARLY) :]:
        moved[c] = lax.ppermute(parts[c], "scan", pairs_of(c))
    arrived = [moved[c] for c in EARLY]
    own = pack_parts(*arrived)
    arrived = smooth_parts(lax.ppermute(own, "col", right), lax.ppermute(own, "col", left), *arrived)
    moved.update(zip(EARLY, arrived))
    moved[0] = parts[0]
    ready = [moved[b - 8] for b in range(FIRST, STOP + 1)]
    result = row_shear(inner_kernel, ready, INNER, (STOP - FIRST) * BLOCK, ())
    rest = [moved[b - 8] for b in list(range(FIRST + 2)) + list(range(STOP - 1, SENDS))]
    full_rows = (FIRST + 1 + SENDS - STOP) * BLOCK + 2 * MARGIN
    return row_shear(outer_kernel, rest, 4 * OUTER, full_rows, (4,), result)


def solution(mesh):
    placed = (P("scan", None, "col"), P("scan"))
    return jax.shard_map(local, mesh=mesh, in_specs=placed, out_specs=P("scan", None, "col"), check_vma=False)
```

```python
import functools

import jax
import jax.numpy as jnp
import numpy as np
from jax import lax
from jax.experimental import pallas as pl
from jax.experimental.pallas import tpu as pltpu
from jax.sharding import PartitionSpec as P

SLAB = 16
ROWS = 2048
COLS = 128
BLOCK = 128
SENDS = ROWS // BLOCK + 1
HALF_SKEW = 894
SCANS = 32
HELD = SLAB + 3
PAD = 128
EDGE_ROWS = 512
MARGIN = 144
VMEM_LIMIT = 60 * 1024 * 1024

ORDER = (4, -4, 8, -8, 3, -3, 7, -7, 5, -5, 1, -1, 2, -2, 6, -6)
EARLY = ORDER[:8]
LATE = ORDER[8:] + (0,)
CODED = ROWS + 16
FIRST, STOP = 5, 11

HBM = pl.BlockSpec(memory_space=pl.ANY)
VMEM = pl.BlockSpec(memory_space=pltpu.VMEM)
SMEM = pl.BlockSpec(memory_space=pltpu.SMEM)

COST = pl.CostEstimate(flops=1000, bytes_accessed=1000, transcendentals=0)


def dot(a, b):
    return jnp.dot(a, b, preferred_element_type=jnp.float32)


def halos_kernel(offsets, raw_ref, first_ref, final_ref, planes, sem, out_sem):
    sides = ((first_ref, 0, 0), (first_ref, 1, 1), (final_ref, 0, SLAB - 1))
    loads = [pltpu.make_async_copy(raw_ref.at[p], planes.at[n, pl.ds(0, ROWS)], sem.at[n]) for n, (_, _, p) in enumerate(sides)]
    for load in loads:
        load.start()
    lane = lax.broadcasted_iota(jnp.int32, (16, COLS), 1)
    for n, (_, _, p) in enumerate(sides):
        shift = offsets[p]
        code = jnp.where(lane == 0, lax.shift_right_logical(shift, 4), jnp.where(lane == 1, shift & 15, 0))
        planes[n, ROWS:CODED, :] = code.astype(jnp.float32).astype(jnp.bfloat16)
    stores = []
    for n, (ref, at, _) in enumerate(sides):
        loads[n].wait()
        stores.append(pltpu.make_async_copy(planes.at[n], ref.at[at], out_sem.at[n]))
        stores[-1].start()
    for store in stores:
        store.wait()


def halos(offsets, raw):
    return pl.pallas_call(
        halos_kernel,
        out_shape=tuple(jax.ShapeDtypeStruct((n, CODED, COLS), jnp.bfloat16) for n in (2, 1)),
        in_specs=[SMEM, HBM],
        out_specs=(HBM, HBM),
        scratch_shapes=[pltpu.VMEM((3, CODED, COLS), jnp.bfloat16), pltpu.SemaphoreType.DMA((3,)), pltpu.SemaphoreType.DMA((3,))],
        cost_estimate=COST,
        name="halos",
    )(offsets, raw)


def pack_edges_kernel(raw_ref, out_ref, planes, sem):
    def fetch(g):
        rows = pl.ds(EDGE_ROWS * g, EDGE_ROWS)
        return pltpu.make_async_copy(raw_ref.at[:, rows], planes.at[:, rows], sem.at[g])

    for g in range(4):
        fetch(g).start()
    src = lax.broadcasted_iota(jnp.int32, (SLAB * COLS, COLS), 0)
    dst = lax.broadcasted_iota(jnp.int32, (SLAB * COLS, COLS), 1)
    pick = (src == COLS * dst + COLS - 1) | (src == COLS * (dst - 16))
    pick = jnp.where(pick & (dst < 32), 1.0, 0.0).astype(jnp.bfloat16)
    total = None
    for g in range(4):
        fetch(g).wait()
        rows = slice(EDGE_ROWS * g, EDGE_ROWS * (g + 1))
        values = jnp.concatenate([planes[p, rows, :] for p in range(SLAB)], axis=1)
        found = dot(values, pick)
        total = found if g == 0 else total + pltpu.roll(found, 32 * g, 1)
    out_ref[...] = total.astype(jnp.bfloat16)


def pack_edges(raw):
    return pl.pallas_call(
        pack_edges_kernel,
        out_shape=jax.ShapeDtypeStruct((EDGE_ROWS, COLS), jnp.bfloat16),
        in_specs=[HBM],
        out_specs=VMEM,
        scratch_shapes=[
            pltpu.VMEM((SLAB, ROWS, COLS), jnp.bfloat16),
            pltpu.SemaphoreType.DMA((4,)),
        ],
        compiler_params=pltpu.CompilerParams(vmem_limit_bytes=VMEM_LIMIT),
        cost_estimate=COST,
        name="pack_edges",
    )(raw)


def column_weights():
    held = np.zeros((SLAB, 2 * COLS, COLS), np.float32)
    for at in range(COLS):
        held[:, at, at] = 0.125
        held[:, at, [n for n in (at - 1, at + 1) if 0 <= n < COLS]] = 0.0625
    for p in range(SLAB):
        for g in range(4):
            held[p, COLS + 32 * g + p, 0] = 0.0625
            held[p, COLS + 32 * g + 16 + p, COLS - 1] = 0.0625
    return jnp.asarray(held, jnp.bfloat16)


def shear_kernel(group, offsets, raw_ref, before_ref, after_ref, *rest):
    count = len(group)
    late = group == LATE
    if late:
        weights_ref, edges_before, edges_own, edges_after, *rest = rest
    outs, rest = rest[:count], rest[count:]
    planes, held, packed, codes, offs, sem, out_sem, code_sem, *rest = rest
    device = lax.axis_index("scan")
    last = device == SCANS - 1
    beside_refs = ((0, before_ref, 0), (SLAB + 1, after_ref, 0), (SLAB + 2, after_ref, 1))

    code_copies = [
        pltpu.make_async_copy(ref.at[p, pl.ds(ROWS, 16)], codes.at[n], code_sem.at[n])
        for n, (_, ref, p) in enumerate(beside_refs)
    ]
    loads = []
    for slot in range(HELD):
        ref, p = (before_ref, 0) if slot == 0 else (raw_ref, slot - 1) if slot <= SLAB else (after_ref, slot - SLAB - 1)
        loads.append(pltpu.make_async_copy(ref.at[p, pl.ds(0, ROWS)], planes.at[slot], sem.at[slot]))
    for load in loads + code_copies:
        load.start()
    for p in range(SLAB):
        offs[p + 1] = offsets[p]
    zeros = jnp.zeros((PAD, COLS), jnp.float32)
    for slot in range(HELD):
        held[slot, 0:PAD, :] = zeros
        held[slot, PAD + ROWS : PAD + ROWS + PAD, :] = zeros
    if late:
        beside, weights, weights_sem = rest
        weights_copy = pltpu.make_async_copy(weights_ref, weights, weights_sem)
        weights_copy.start()
        lane = lax.broadcasted_iota(jnp.int32, (EDGE_ROWS, COLS), 1)
        for e, edges in enumerate((edges_before, edges_own, edges_after)):
            values = edges[...].astype(jnp.float32)
            for g in range(4):
                mine = (lane >= 32 * g) & (lane < 32 * g + 32)
                beside[e, EDGE_ROWS * g : EDGE_ROWS * (g + 1), :] = jnp.where(mine, values, 0.0).astype(jnp.bfloat16)
        weights_copy.wait()
    for slot in range(HELD):
        loads[slot].wait()
        if late:
            e = 0 if slot == 0 else 1 if slot <= SLAB else 2
            values = jnp.concatenate([planes[slot], beside[e]], axis=1)
            held[slot, PAD : PAD + ROWS, :] = dot(values, weights[(slot + SLAB - 1) % SLAB])
        else:
            held[slot, PAD : PAD + ROWS, :] = planes[slot].astype(jnp.float32) * 0.25
    row = lax.broadcasted_iota(jnp.int32, (16, COLS), 0)
    lane = lax.broadcasted_iota(jnp.int32, (16, COLS), 1)
    scale = jnp.where(row == 0, jnp.where(lane == 0, 16.0, jnp.where(lane == 1, 1.0, 0.0)), 0.0)
    for n, (slot, _, _) in enumerate(beside_refs):
        code_copies[n].wait()
        offs[slot] = jnp.sum(codes[n].astype(jnp.float32) * scale).astype(jnp.int32)

    def block_of(i):
        found = jnp.int32(group[0] + 8)
        for at, c in enumerate(group[1:]):
            found = jnp.where(i == at + 1, c + 8, found)
        return found

    share = (2 * lax.broadcasted_iota(jnp.int32, (8, COLS), 0) + 1).astype(jnp.float32) * 0.0625

    def send(i, _):
        b = block_of(i)
        low = b < SENDS // 2
        role = jnp.logical_and(last, low)
        end = jnp.logical_and(last, jnp.logical_not(low))
        keep_15 = jnp.where(role, 0.0, 1.0).astype(jnp.float32)
        keep_16 = jnp.where(end, 0.0, 1.0).astype(jnp.float32)

        def starts(block, none):
            found = []
            for slot in range(HELD):
                dead = jnp.logical_or(none, role if slot <= SLAB else end)
                start = jnp.clip(PAD + HALF_SKEW + block * BLOCK - offs[slot], 0, PAD + ROWS)
                found.append(jnp.where(dead, 0, start))
            return found

        here = starts(b, b == SENDS - 1)
        above = starts(b - 1, b == 0)

        def mixed(r, bases, first, stop):
            x = {p: held[p + 1, pl.ds(bases[p + 1] + 8 * r, 8), :] for p in range(first - 1, stop + 2)}
            v = {p: x[p] + x[p + 1] for p in range(first - 1, stop + 1)}
            u = {}
            for p in range(first, stop + 1):
                u[p] = v[p - 1] + v[p]
                if p == SLAB - 1:
                    u[p] = u[p] * keep_15
                if p == SLAB:
                    u[p] = u[p] * keep_16
            return {p: u[p] + share * (u[p + 1] - u[p]) for p in range(first, stop)}

        def both(r):
            got = dict(mixed(r, here, r, SLAB))
            if r:
                got.update({p + SLAB: v for p, v in mixed(r, above, 0, r).items()})
            got = [got[q + r] for q in range(SLAB)]
            return got

        for t in range(8):
            even, odd = both(2 * t), both(2 * t + 1)
            for q in range(SLAB):
                tile = jnp.concatenate([even[q], odd[q]], axis=0)
                packed[i, q, 16 * t : 16 * t + 16, :] = tile.astype(jnp.bfloat16)
        for at in range(count):

            @pl.when(i == at)
            def _():
                pltpu.make_async_copy(packed.at[at], outs[at], out_sem.at[at]).start()

        return 0

    lax.fori_loop(0, count, send, 0)
    for at in range(count):
        pltpu.make_async_copy(packed.at[at], outs[at], out_sem.at[at]).wait()


PART = jax.ShapeDtypeStruct((SLAB, BLOCK, COLS), jnp.bfloat16)


def shear(group, *operands):
    count = len(group)
    late = group == LATE
    extra = [
        pltpu.VMEM((3, ROWS, COLS), jnp.bfloat16),
        pltpu.VMEM((SLAB, 2 * COLS, COLS), jnp.bfloat16),
        pltpu.SemaphoreType.DMA,
    ]
    return pl.pallas_call(
        functools.partial(shear_kernel, group),
        out_shape=(PART,) * count,
        in_specs=[SMEM, HBM, HBM, HBM] + ([HBM, VMEM, VMEM, VMEM] if late else []),
        out_specs=(HBM,) * count,
        scratch_shapes=[
            pltpu.VMEM((HELD, ROWS, COLS), jnp.bfloat16),
            pltpu.VMEM((HELD, PAD + ROWS + PAD, COLS), jnp.float32),
            pltpu.VMEM((count, SLAB, BLOCK, COLS), jnp.bfloat16),
            pltpu.VMEM((3, 16, COLS), jnp.bfloat16),
            pltpu.SMEM((HELD,), jnp.int32),
            pltpu.SemaphoreType.DMA((HELD,)),
            pltpu.SemaphoreType.DMA((count,)),
            pltpu.SemaphoreType.DMA((3,)),
        ]
        + (extra if late else []),
        compiler_params=pltpu.CompilerParams(vmem_limit_bytes=VMEM_LIMIT),
        cost_estimate=COST,
        name="shear_planes",
    )(*operands)


def pack_parts_kernel(*refs):
    parts, out_ref = refs[:-1], refs[-1]
    pair = lax.shift_right_logical(lax.broadcasted_iota(jnp.int32, (16, COLS), 1), 1)
    for first in range(0, len(parts), 4):
        for t in range(8):
            rows = slice(16 * t, 16 * t + 16)
            total = jnp.zeros((16, COLS), jnp.float32)
            for n, part in enumerate(parts[first : first + 4]):
                for q in range(SLAB):
                    found = pltpu.roll(part[q, rows, :].astype(jnp.float32), (32 * n + 2 * q + 1) % COLS, 1)
                    total = jnp.where(pair == 16 * n + q, found, total)
            out_ref[32 * first + 16 * t : 32 * first + 16 * t + 16, :] = total.astype(jnp.bfloat16)


def pack_parts(*parts):
    return pl.pallas_call(
        pack_parts_kernel,
        out_shape=jax.ShapeDtypeStruct((BLOCK * len(parts) // 4, COLS), jnp.bfloat16),
        in_specs=[VMEM] * len(parts),
        out_specs=VMEM,
        compiler_params=pltpu.CompilerParams(vmem_limit_bytes=VMEM_LIMIT),
        cost_estimate=COST,
        name="pack_parts",
    )(*parts)


def smooth_parts_kernel(from_left, from_right, *refs):
    count = len(refs) // 2
    parts, outs = refs[:count], refs[count:]
    src = lax.broadcasted_iota(jnp.int32, (COLS, COLS), 0)
    dst = lax.broadcasted_iota(jnp.int32, (COLS, COLS), 1)
    tri = jnp.where(src == dst, 0.5, jnp.where(jnp.abs(src - dst) == 1, 0.25, 0.0)).astype(jnp.bfloat16)
    left_lane = (lax.broadcasted_iota(jnp.int32, from_left.shape, 1) & 1) == 0
    edges = jnp.where(left_lane, from_left[...].astype(jnp.float32), from_right[...].astype(jnp.float32)).astype(jnp.bfloat16)
    for n in range(count):
        for q in range(SLAB):
            lane = 32 * (n % 4) + 2 * q
            hit = ((src == lane) & (dst == 0)) | ((src == lane + 1) & (dst == COLS - 1))
            weights = jnp.concatenate([tri, jnp.where(hit, 0.25, 0.0).astype(jnp.bfloat16)], axis=0)
            values = jnp.concatenate([parts[n][q], edges[BLOCK * (n // 4) : BLOCK * (n // 4 + 1)]], axis=1)
            outs[n][q] = dot(values, weights).astype(jnp.bfloat16)


def smooth_parts(from_left, from_right, *parts):
    return pl.pallas_call(
        smooth_parts_kernel,
        out_shape=(jax.ShapeDtypeStruct((SLAB, BLOCK, COLS), jnp.bfloat16),) * len(parts),
        in_specs=[VMEM] * (2 + len(parts)),
        out_specs=(VMEM,) * len(parts),
        compiler_params=pltpu.CompilerParams(vmem_limit_bytes=VMEM_LIMIT),
        cost_estimate=COST,
        name="smooth_parts",
    )(from_left, from_right, *parts)


def merge(got, full, at, blocks, top):
    upper = lax.broadcasted_iota(jnp.int32, (16, COLS), 0) < 8

    def one(b, _):
        for q in range(SLAB):
            for t in range(8):
                rows = slice(16 * t, 16 * t + 16)
                if q + 2 * t + 1 < SLAB:
                    tile = got[at + b, q, rows, :].astype(jnp.float32)
                elif q + 2 * t >= SLAB:
                    tile = got[at + b + 1, q, rows, :].astype(jnp.float32)
                else:
                    ours = got[at + b, q, rows, :].astype(jnp.float32)
                    tile = jnp.where(upper, ours, got[at + b + 1, q, rows, :].astype(jnp.float32))
                full[q, pl.ds(pl.multiple_of(top + b * BLOCK + 16 * t, 16), 16), :] = tile
        return 0

    lax.fori_loop(0, blocks, one, 0)


def shift_of(q):
    numerator = 17 * (2 * (lax.axis_index("scan") * SLAB + q) - (SLAB * SCANS - 1))
    whole = lax.shift_right_arithmetic(numerator, 6)
    share = (numerator & 63).astype(jnp.float32) * (1.0 / 64.0)
    tile = -lax.shift_right_arithmetic(whole, 4)
    return whole, share, tile


def interpolate(full, done, q, source, target, tiles, share):
    for t in range(tiles):
        a = full[q, pl.ds(source + 16 * t, 16), :]
        c = full[q, pl.ds(source + 1 + 16 * t, 16), :]
        done[q, pl.ds(pl.multiple_of(target + 16 * t, 16), 16), :] = (a + share * (c - a)).astype(jnp.bfloat16)


INNER = (STOP - FIRST) * BLOCK - 16
OUTER = 400
LOW = FIRST * BLOCK
LAG = 8
HIGH = LOW + INNER


INNER_PARTS = [c for c in ORDER + (0,) if FIRST <= c + 8 <= STOP]
OUTER_PARTS = [c for c in ORDER + (0,) if c + 8 <= FIRST + 1 or c + 8 >= STOP - 1]


def inner_kernel(*refs):
    count = STOP - FIRST + 1
    parts = [refs[INNER_PARTS.index(b - 8)] for b in range(FIRST, STOP + 1)]
    out_ref, got, full, done, sem, out_sem = refs[count:]

    def fetch(i):
        return pltpu.make_async_copy(parts[i], got.at[i], sem.at[i])

    for i in range(count):
        fetch(i).start()
    for i in range(count):
        fetch(i).wait()
    merge(got, full, 0, STOP - FIRST, 0)

    def put(q, tile):
        return pltpu.make_async_copy(done.at[q], out_ref.at[q, pl.ds(pl.multiple_of(LOW + 16 * tile, 16), INNER)], out_sem.at[q])

    def plane(q, _):
        whole, share, tile = shift_of(q)
        interpolate(full, done, q, 16 * tile + whole, 0, INNER // 16, share)
        put(q, tile).start()
        return 0

    lax.fori_loop(0, SLAB, plane, 0)
    for q in range(SLAB):
        put(q, shift_of(q)[2]).wait()


def outer_kernel(*refs):
    top, bottom = FIRST + 2, SENDS - STOP + 1
    count = top + bottom
    wanted = list(range(top)) + list(range(STOP - 1, SENDS))
    parts = [refs[OUTER_PARTS.index(b - 8)] for b in wanted]
    _, out_ref, got, full, done, sem, out_sem = refs[count:]

    def fetch(i):
        return pltpu.make_async_copy(parts[i], got.at[i], sem.at[i])

    for i in range(count):
        fetch(i).start()
    zeros = jnp.zeros((MARGIN, COLS), jnp.float32)
    low_rows, high_rows = (top - 1) * BLOCK, (bottom - 1) * BLOCK
    base = MARGIN + low_rows
    first_row = ROWS - high_rows

    def clear(q, _):
        full[q, 0:MARGIN, :] = zeros
        full[q, base + high_rows : base + high_rows + MARGIN, :] = zeros
        return 0

    lax.fori_loop(0, SLAB, clear, 0)
    for i in range(count):
        fetch(i).wait()
    merge(got, full, 0, top - 1, MARGIN)
    merge(got, full, top, bottom - 1, base)

    def targets(tile):
        low = jnp.maximum(LOW + 16 * tile - OUTER, 0)
        high = jnp.minimum(HIGH + 16 * tile, ROWS - OUTER)
        return 0, low, high, ROWS - OUTER

    def puts(q, tile):
        return [
            pltpu.make_async_copy(
                done.at[q, pl.ds(OUTER * n, OUTER)], out_ref.at[q, pl.ds(pl.multiple_of(row, 16), OUTER)], out_sem.at[q, n]
            )
            for n, row in enumerate(targets(tile))
        ]

    def plane(q, _):
        whole, share, tile = shift_of(q)
        for n, row in enumerate(targets(tile)):
            source = row + whole + (MARGIN if n < 2 else base - first_row)
            interpolate(full, done, q, source, OUTER * n, OUTER // 16, share)
        for put in puts(q, tile)[::3]:
            put.start()

        @pl.when(q >= LAG)
        def _():
            inward(q - LAG)

        return 0

    def inward(q):
        first, low, high, final = puts(q, shift_of(q)[2])
        first.wait()
        final.wait()
        low.start()
        high.start()

    lax.fori_loop(0, SLAB, plane, 0)
    for q in range(SLAB - LAG, SLAB):
        inward(q)
    for q in range(SLAB):
        for put in puts(q, shift_of(q)[2])[1:3]:
            put.wait()


def row_shear(kernel, parts, rows, full_rows, puts, into=None):
    count = len(parts)
    operands = list(parts) + ([] if into is None else [into])
    return pl.pallas_call(
        kernel,
        out_shape=jax.ShapeDtypeStruct((SLAB, ROWS, COLS), jnp.bfloat16),
        in_specs=[HBM] * len(operands),
        out_specs=HBM,
        scratch_shapes=[
            pltpu.VMEM((count, SLAB, BLOCK, COLS), jnp.bfloat16),
            pltpu.VMEM((SLAB, full_rows, COLS), jnp.float32),
            pltpu.VMEM((SLAB, rows, COLS), jnp.bfloat16),
            pltpu.SemaphoreType.DMA((count,)),
            pltpu.SemaphoreType.DMA((SLAB,) + puts),
        ],
        input_output_aliases={} if into is None else {count: 0},
        compiler_params=pltpu.CompilerParams(vmem_limit_bytes=VMEM_LIMIT),
        cost_estimate=COST,
        name="shear_rows",
    )(*operands)


def pairs_of(c):
    found = [(s, s - c) for s in range(SCANS) if 0 <= s - c < SCANS]
    if c < 0:
        found.append((SCANS - 1, -c - 1))
    return found


def local(raw, offsets):
    up = [(i, i + 1) for i in range(SCANS - 1)]
    down = [((i + 1) % SCANS, i) for i in range(SCANS)]
    right = [(i, i + 1) for i in range(3)]
    left = [(i + 1, i) for i in range(3)]
    first, final = halos(offsets, raw)
    after = lax.ppermute(first, "scan", down)
    before = lax.ppermute(final, "scan", up)
    own = pack_edges(raw)
    from_left = lax.ppermute(own, "col", right)
    from_right = lax.ppermute(own, "col", left)
    raw, _ = lax.optimization_barrier((raw, own))
    made = shear(EARLY, offsets, raw, before, after)
    moved = {c: lax.ppermute(part, "scan", pairs_of(c)) for c, part in zip(EARLY, made)}
    lane = lax.broadcasted_iota(jnp.int32, own.shape, 1)
    edges = jnp.where(lane % 32 < 16, from_left, from_right)
    edges, _ = lax.optimization_barrier((edges, made[0]))
    edges_after = lax.ppermute(edges, "scan", down)
    edges_before = lax.ppermute(edges, "scan", up)
    made = shear(LATE, offsets, raw, before, after, column_weights(), edges_before, edges, edges_after)
    parts = dict(zip(LATE, made))
    for c in ORDER[len(EARLY) :]:
        moved[c] = lax.ppermute(parts[c], "scan", pairs_of(c))
    arrived = [moved[c] for c in EARLY]
    own = pack_parts(*arrived)
    arrived = smooth_parts(lax.ppermute(own, "col", right), lax.ppermute(own, "col", left), *arrived)
    moved.update(zip(EARLY, arrived))
    moved[0] = parts[0]
    sooner = ORDER[:-2]
    moved.update(zip(sooner, lax.optimization_barrier([moved[c] for c in sooner])))
    ready = [moved[c] for c in INNER_PARTS]
    result = row_shear(inner_kernel, ready, INNER, (STOP - FIRST) * BLOCK, ())
    rest = [moved[c] for c in OUTER_PARTS]
    full_rows = (FIRST + 1 + SENDS - STOP) * BLOCK + 2 * MARGIN
    return row_shear(outer_kernel, rest, 4 * OUTER, full_rows, (4,), result)


def solution(mesh):
    placed = (P("scan", None, "col"), P("scan"))
    return jax.shard_map(local, mesh=mesh, in_specs=placed, out_specs=P("scan", None, "col"), check_vma=False)
```

```python
import functools

import jax
import jax.numpy as jnp
import numpy as np
from jax import lax
from jax.experimental import pallas as pl
from jax.experimental.pallas import tpu as pltpu
from jax.sharding import PartitionSpec as P

SLAB = 16
ROWS = 2048
COLS = 128
BLOCK = 128
SENDS = ROWS // BLOCK + 1
HALF_SKEW = 894
SCANS = 32
HELD = SLAB + 3
PAD = 128
EDGE_ROWS = 512
MARGIN = 144
VMEM_LIMIT = 60 * 1024 * 1024

ORDER = (4, -4, 8, -8, 3, -3, 7, -7, 5, -5, 2, -2, 1, -1, 6, -6)
EARLY = ORDER[:8]
LATE = ORDER[8:] + (0,)
CODED = ROWS + 16
FIRST, STOP = 5, 11

HBM = pl.BlockSpec(memory_space=pl.ANY)
VMEM = pl.BlockSpec(memory_space=pltpu.VMEM)
SMEM = pl.BlockSpec(memory_space=pltpu.SMEM)

COST = pl.CostEstimate(flops=1000, bytes_accessed=1000, transcendentals=0)


def dot(a, b):
    return jnp.dot(a, b, preferred_element_type=jnp.float32)


def halos_kernel(offsets, raw_ref, first_ref, final_ref, planes, sem, out_sem):
    sides = ((first_ref, 0, 0), (first_ref, 1, 1), (final_ref, 0, SLAB - 1))
    loads = [pltpu.make_async_copy(raw_ref.at[p], planes.at[n, pl.ds(0, ROWS)], sem.at[n]) for n, (_, _, p) in enumerate(sides)]
    for load in loads:
        load.start()
    lane = lax.broadcasted_iota(jnp.int32, (16, COLS), 1)
    for n, (_, _, p) in enumerate(sides):
        shift = offsets[p]
        code = jnp.where(lane == 0, lax.shift_right_logical(shift, 4), jnp.where(lane == 1, shift & 15, 0))
        planes[n, ROWS:CODED, :] = code.astype(jnp.float32).astype(jnp.bfloat16)
    stores = []
    for n, (ref, at, _) in enumerate(sides):
        loads[n].wait()
        stores.append(pltpu.make_async_copy(planes.at[n], ref.at[at], out_sem.at[n]))
        stores[-1].start()
    for store in stores:
        store.wait()


def halos(offsets, raw):
    return pl.pallas_call(
        halos_kernel,
        out_shape=tuple(jax.ShapeDtypeStruct((n, CODED, COLS), jnp.bfloat16) for n in (2, 1)),
        in_specs=[SMEM, HBM],
        out_specs=(HBM, HBM),
        scratch_shapes=[pltpu.VMEM((3, CODED, COLS), jnp.bfloat16), pltpu.SemaphoreType.DMA((3,)), pltpu.SemaphoreType.DMA((3,))],
        cost_estimate=COST,
        name="halos",
    )(offsets, raw)


def pack_edges_kernel(raw_ref, out_ref, planes, sem):
    def fetch(g):
        rows = pl.ds(EDGE_ROWS * g, EDGE_ROWS)
        return pltpu.make_async_copy(raw_ref.at[:, rows], planes.at[:, rows], sem.at[g])

    for g in range(4):
        fetch(g).start()
    src = lax.broadcasted_iota(jnp.int32, (SLAB * COLS, COLS), 0)
    dst = lax.broadcasted_iota(jnp.int32, (SLAB * COLS, COLS), 1)
    pick = (src == COLS * dst + COLS - 1) | (src == COLS * (dst - 16))
    pick = jnp.where(pick & (dst < 32), 1.0, 0.0).astype(jnp.bfloat16)
    total = None
    for g in range(4):
        fetch(g).wait()
        rows = slice(EDGE_ROWS * g, EDGE_ROWS * (g + 1))
        values = jnp.concatenate([planes[p, rows, :] for p in range(SLAB)], axis=1)
        found = dot(values, pick)
        total = found if g == 0 else total + pltpu.roll(found, 32 * g, 1)
    out_ref[...] = total.astype(jnp.bfloat16)


def pack_edges(raw):
    return pl.pallas_call(
        pack_edges_kernel,
        out_shape=jax.ShapeDtypeStruct((EDGE_ROWS, COLS), jnp.bfloat16),
        in_specs=[HBM],
        out_specs=VMEM,
        scratch_shapes=[
            pltpu.VMEM((SLAB, ROWS, COLS), jnp.bfloat16),
            pltpu.SemaphoreType.DMA((4,)),
        ],
        compiler_params=pltpu.CompilerParams(vmem_limit_bytes=VMEM_LIMIT),
        cost_estimate=COST,
        name="pack_edges",
    )(raw)


def column_weights():
    held = np.zeros((SLAB, 2 * COLS, COLS), np.float32)
    for at in range(COLS):
        held[:, at, at] = 0.125
        held[:, at, [n for n in (at - 1, at + 1) if 0 <= n < COLS]] = 0.0625
    for p in range(SLAB):
        for g in range(4):
            held[p, COLS + 32 * g + p, 0] = 0.0625
            held[p, COLS + 32 * g + 16 + p, COLS - 1] = 0.0625
    return jnp.asarray(held, jnp.bfloat16)


def shear_kernel(group, offsets, raw_ref, before_ref, after_ref, *rest):
    count = len(group)
    late = group == LATE
    if late:
        weights_ref, edges_before, edges_own, edges_after, *rest = rest
    outs, rest = rest[:count], rest[count:]
    planes, held, packed, codes, offs, sem, out_sem, code_sem, *rest = rest
    device = lax.axis_index("scan")
    last = device == SCANS - 1
    beside_refs = ((0, before_ref, 0), (SLAB + 1, after_ref, 0), (SLAB + 2, after_ref, 1))

    code_copies = [
        pltpu.make_async_copy(ref.at[p, pl.ds(ROWS, 16)], codes.at[n], code_sem.at[n])
        for n, (_, ref, p) in enumerate(beside_refs)
    ]
    loads = []
    for slot in range(HELD):
        ref, p = (before_ref, 0) if slot == 0 else (raw_ref, slot - 1) if slot <= SLAB else (after_ref, slot - SLAB - 1)
        loads.append(pltpu.make_async_copy(ref.at[p, pl.ds(0, ROWS)], planes.at[slot], sem.at[slot]))
    for load in loads + code_copies:
        load.start()
    for p in range(SLAB):
        offs[p + 1] = offsets[p]
    zeros = jnp.zeros((PAD, COLS), jnp.float32)
    for slot in range(HELD):
        held[slot, 0:PAD, :] = zeros
        held[slot, PAD + ROWS : PAD + ROWS + PAD, :] = zeros
    if late:
        beside, weights, weights_sem = rest
        weights_copy = pltpu.make_async_copy(weights_ref, weights, weights_sem)
        weights_copy.start()
        lane = lax.broadcasted_iota(jnp.int32, (EDGE_ROWS, COLS), 1)
        for e, edges in enumerate((edges_before, edges_own, edges_after)):
            values = edges[...].astype(jnp.float32)
            for g in range(4):
                mine = (lane >= 32 * g) & (lane < 32 * g + 32)
                beside[e, EDGE_ROWS * g : EDGE_ROWS * (g + 1), :] = jnp.where(mine, values, 0.0).astype(jnp.bfloat16)
        weights_copy.wait()
    for slot in range(HELD):
        loads[slot].wait()
        if late:
            e = 0 if slot == 0 else 1 if slot <= SLAB else 2
            values = jnp.concatenate([planes[slot], beside[e]], axis=1)
            held[slot, PAD : PAD + ROWS, :] = dot(values, weights[(slot + SLAB - 1) % SLAB])
        else:
            held[slot, PAD : PAD + ROWS, :] = planes[slot].astype(jnp.float32) * 0.25
    row = lax.broadcasted_iota(jnp.int32, (16, COLS), 0)
    lane = lax.broadcasted_iota(jnp.int32, (16, COLS), 1)
    scale = jnp.where(row == 0, jnp.where(lane == 0, 16.0, jnp.where(lane == 1, 1.0, 0.0)), 0.0)
    for n, (slot, _, _) in enumerate(beside_refs):
        code_copies[n].wait()
        offs[slot] = jnp.sum(codes[n].astype(jnp.float32) * scale).astype(jnp.int32)

    def block_of(i):
        found = jnp.int32(group[0] + 8)
        for at, c in enumerate(group[1:]):
            found = jnp.where(i == at + 1, c + 8, found)
        return found

    share = (2 * lax.broadcasted_iota(jnp.int32, (8, COLS), 0) + 1).astype(jnp.float32) * 0.0625

    def send(i, _):
        b = block_of(i)
        low = b < SENDS // 2
        role = jnp.logical_and(last, low)
        end = jnp.logical_and(last, jnp.logical_not(low))
        keep_15 = jnp.where(role, 0.0, 1.0).astype(jnp.float32)
        keep_16 = jnp.where(end, 0.0, 1.0).astype(jnp.float32)

        def starts(block, none):
            found = []
            for slot in range(HELD):
                dead = jnp.logical_or(none, role if slot <= SLAB else end)
                start = jnp.clip(PAD + HALF_SKEW + block * BLOCK - offs[slot], 0, PAD + ROWS)
                found.append(jnp.where(dead, 0, start))
            return found

        here = starts(b, b == SENDS - 1)
        above = starts(b - 1, b == 0)

        def mixed(r, bases, first, stop):
            x = {p: held[p + 1, pl.ds(bases[p + 1] + 8 * r, 8), :] for p in range(first - 1, stop + 2)}
            v = {p: x[p] + x[p + 1] for p in range(first - 1, stop + 1)}
            u = {}
            for p in range(first, stop + 1):
                u[p] = v[p - 1] + v[p]
                if p == SLAB - 1:
                    u[p] = u[p] * keep_15
                if p == SLAB:
                    u[p] = u[p] * keep_16
            return {p: u[p] + share * (u[p + 1] - u[p]) for p in range(first, stop)}

        def both(r):
            got = dict(mixed(r, here, r, SLAB))
            if r:
                got.update({p + SLAB: v for p, v in mixed(r, above, 0, r).items()})
            got = [got[q + r] for q in range(SLAB)]
            return got

        for t in range(8):
            even, odd = both(2 * t), both(2 * t + 1)
            for q in range(SLAB):
                tile = jnp.concatenate([even[q], odd[q]], axis=0)
                packed[i, q, 16 * t : 16 * t + 16, :] = tile.astype(jnp.bfloat16)
        for at in range(count):

            @pl.when(i == at)
            def _():
                pltpu.make_async_copy(packed.at[at], outs[at], out_sem.at[at]).start()

        return 0

    lax.fori_loop(0, count, send, 0)
    for at in range(count):
        pltpu.make_async_copy(packed.at[at], outs[at], out_sem.at[at]).wait()


PART = jax.ShapeDtypeStruct((SLAB, BLOCK, COLS), jnp.bfloat16)


def shear(group, *operands):
    count = len(group)
    late = group == LATE
    extra = [
        pltpu.VMEM((3, ROWS, COLS), jnp.bfloat16),
        pltpu.VMEM((SLAB, 2 * COLS, COLS), jnp.bfloat16),
        pltpu.SemaphoreType.DMA,
    ]
    return pl.pallas_call(
        functools.partial(shear_kernel, group),
        out_shape=(PART,) * count,
        in_specs=[SMEM, HBM, HBM, HBM] + ([HBM, VMEM, VMEM, VMEM] if late else []),
        out_specs=(HBM,) * count,
        scratch_shapes=[
            pltpu.VMEM((HELD, ROWS, COLS), jnp.bfloat16),
            pltpu.VMEM((HELD, PAD + ROWS + PAD, COLS), jnp.float32),
            pltpu.VMEM((count, SLAB, BLOCK, COLS), jnp.bfloat16),
            pltpu.VMEM((3, 16, COLS), jnp.bfloat16),
            pltpu.SMEM((HELD,), jnp.int32),
            pltpu.SemaphoreType.DMA((HELD,)),
            pltpu.SemaphoreType.DMA((count,)),
            pltpu.SemaphoreType.DMA((3,)),
        ]
        + (extra if late else []),
        compiler_params=pltpu.CompilerParams(vmem_limit_bytes=VMEM_LIMIT),
        cost_estimate=COST,
        name="shear_planes",
    )(*operands)


def pack_parts_kernel(*refs):
    parts, out_ref = refs[:-1], refs[-1]
    pair = lax.shift_right_logical(lax.broadcasted_iota(jnp.int32, (16, COLS), 1), 1)
    for first in range(0, len(parts), 4):
        for t in range(8):
            rows = slice(16 * t, 16 * t + 16)
            total = jnp.zeros((16, COLS), jnp.float32)
            for n, part in enumerate(parts[first : first + 4]):
                for q in range(SLAB):
                    found = pltpu.roll(part[q, rows, :].astype(jnp.float32), (32 * n + 2 * q + 1) % COLS, 1)
                    total = jnp.where(pair == 16 * n + q, found, total)
            out_ref[32 * first + 16 * t : 32 * first + 16 * t + 16, :] = total.astype(jnp.bfloat16)


def pack_parts(*parts):
    return pl.pallas_call(
        pack_parts_kernel,
        out_shape=jax.ShapeDtypeStruct((BLOCK * len(parts) // 4, COLS), jnp.bfloat16),
        in_specs=[VMEM] * len(parts),
        out_specs=VMEM,
        compiler_params=pltpu.CompilerParams(vmem_limit_bytes=VMEM_LIMIT),
        cost_estimate=COST,
        name="pack_parts",
    )(*parts)


def smooth_parts_kernel(from_left, from_right, *refs):
    count = len(refs) // 2
    parts, outs = refs[:count], refs[count:]
    src = lax.broadcasted_iota(jnp.int32, (COLS, COLS), 0)
    dst = lax.broadcasted_iota(jnp.int32, (COLS, COLS), 1)
    tri = jnp.where(src == dst, 0.5, jnp.where(jnp.abs(src - dst) == 1, 0.25, 0.0)).astype(jnp.bfloat16)
    left_lane = (lax.broadcasted_iota(jnp.int32, from_left.shape, 1) & 1) == 0
    edges = jnp.where(left_lane, from_left[...].astype(jnp.float32), from_right[...].astype(jnp.float32)).astype(jnp.bfloat16)
    for n in range(count):
        for q in range(SLAB):
            lane = 32 * (n % 4) + 2 * q
            hit = ((src == lane) & (dst == 0)) | ((src == lane + 1) & (dst == COLS - 1))
            weights = jnp.concatenate([tri, jnp.where(hit, 0.25, 0.0).astype(jnp.bfloat16)], axis=0)
            values = jnp.concatenate([parts[n][q], edges[BLOCK * (n // 4) : BLOCK * (n // 4 + 1)]], axis=1)
            outs[n][q] = dot(values, weights).astype(jnp.bfloat16)


def smooth_parts(from_left, from_right, *parts):
    return pl.pallas_call(
        smooth_parts_kernel,
        out_shape=(jax.ShapeDtypeStruct((SLAB, BLOCK, COLS), jnp.bfloat16),) * len(parts),
        in_specs=[VMEM] * (2 + len(parts)),
        out_specs=(VMEM,) * len(parts),
        compiler_params=pltpu.CompilerParams(vmem_limit_bytes=VMEM_LIMIT),
        cost_estimate=COST,
        name="smooth_parts",
    )(from_left, from_right, *parts)


def merge(got, full, at, blocks, top):
    upper = lax.broadcasted_iota(jnp.int32, (16, COLS), 0) < 8

    def one(b, _):
        for q in range(SLAB):
            for t in range(8):
                rows = slice(16 * t, 16 * t + 16)
                if q + 2 * t + 1 < SLAB:
                    tile = got[at + b, q, rows, :].astype(jnp.float32)
                elif q + 2 * t >= SLAB:
                    tile = got[at + b + 1, q, rows, :].astype(jnp.float32)
                else:
                    ours = got[at + b, q, rows, :].astype(jnp.float32)
                    tile = jnp.where(upper, ours, got[at + b + 1, q, rows, :].astype(jnp.float32))
                full[q, pl.ds(pl.multiple_of(top + b * BLOCK + 16 * t, 16), 16), :] = tile
        return 0

    lax.fori_loop(0, blocks, one, 0)


def shift_of(q):
    numerator = 17 * (2 * (lax.axis_index("scan") * SLAB + q) - (SLAB * SCANS - 1))
    whole = lax.shift_right_arithmetic(numerator, 6)
    share = (numerator & 63).astype(jnp.float32) * (1.0 / 64.0)
    tile = -lax.shift_right_arithmetic(whole, 4)
    return whole, share, tile


def interpolate(full, done, q, source, target, tiles, share):
    for t in range(tiles):
        a = full[q, pl.ds(source + 16 * t, 16), :]
        c = full[q, pl.ds(source + 1 + 16 * t, 16), :]
        done[q, pl.ds(pl.multiple_of(target + 16 * t, 16), 16), :] = (a + share * (c - a)).astype(jnp.bfloat16)


INNER = (STOP - FIRST) * BLOCK - 16
OUTER = 400
LOW = FIRST * BLOCK
LAG = 8
HIGH = LOW + INNER


INNER_PARTS = [c for c in ORDER + (0,) if FIRST <= c + 8 <= STOP]
OUTER_PARTS = [c for c in ORDER + (0,) if c + 8 <= FIRST + 1 or c + 8 >= STOP - 1]


def inner_kernel(*refs):
    count = STOP - FIRST + 1
    parts = [refs[INNER_PARTS.index(b - 8)] for b in range(FIRST, STOP + 1)]
    out_ref, got, full, done, sem, out_sem = refs[count:]

    def fetch(i):
        return pltpu.make_async_copy(parts[i], got.at[i], sem.at[i])

    for i in range(count):
        fetch(i).start()
    for i in range(count):
        fetch(i).wait()
    merge(got, full, 0, STOP - FIRST, 0)

    def put(q, tile):
        return pltpu.make_async_copy(done.at[q], out_ref.at[q, pl.ds(pl.multiple_of(LOW + 16 * tile, 16), INNER)], out_sem.at[q])

    def plane(q, _):
        whole, share, tile = shift_of(q)
        interpolate(full, done, q, 16 * tile + whole, 0, INNER // 16, share)
        put(q, tile).start()
        return 0

    lax.fori_loop(0, SLAB, plane, 0)
    for q in range(SLAB):
        put(q, shift_of(q)[2]).wait()


def outer_kernel(*refs):
    top, bottom = FIRST + 2, SENDS - STOP + 1
    count = top + bottom
    wanted = list(range(top)) + list(range(STOP - 1, SENDS))
    parts = [refs[OUTER_PARTS.index(b - 8)] for b in wanted]
    _, out_ref, got, full, done, sem, out_sem = refs[count:]

    def fetch(i):
        return pltpu.make_async_copy(parts[i], got.at[i], sem.at[i])

    for i in range(count):
        fetch(i).start()
    zeros = jnp.zeros((MARGIN, COLS), jnp.float32)
    low_rows, high_rows = (top - 1) * BLOCK, (bottom - 1) * BLOCK
    base = MARGIN + low_rows
    first_row = ROWS - high_rows

    def clear(q, _):
        full[q, 0:MARGIN, :] = zeros
        full[q, base + high_rows : base + high_rows + MARGIN, :] = zeros
        return 0

    lax.fori_loop(0, SLAB, clear, 0)
    for i in range(count):
        fetch(i).wait()
    merge(got, full, 0, top - 1, MARGIN)
    merge(got, full, top, bottom - 1, base)

    def targets(tile):
        low = jnp.maximum(LOW + 16 * tile - OUTER, 0)
        high = jnp.minimum(HIGH + 16 * tile, ROWS - OUTER)
        return 0, low, high, ROWS - OUTER

    def puts(q, tile):
        return [
            pltpu.make_async_copy(
                done.at[q, pl.ds(OUTER * n, OUTER)], out_ref.at[q, pl.ds(pl.multiple_of(row, 16), OUTER)], out_sem.at[q, n]
            )
            for n, row in enumerate(targets(tile))
        ]

    def plane(q, _):
        whole, share, tile = shift_of(q)
        for n, row in enumerate(targets(tile)):
            source = row + whole + (MARGIN if n < 2 else base - first_row)
            interpolate(full, done, q, source, OUTER * n, OUTER // 16, share)
        for put in puts(q, tile)[::3]:
            put.start()

        @pl.when(q >= LAG)
        def _():
            inward(q - LAG)

        return 0

    def inward(q):
        first, low, high, final = puts(q, shift_of(q)[2])
        first.wait()
        final.wait()
        low.start()
        high.start()

    lax.fori_loop(0, SLAB, plane, 0)
    for q in range(SLAB - LAG, SLAB):
        inward(q)
    for q in range(SLAB):
        for put in puts(q, shift_of(q)[2])[1:3]:
            put.wait()


def row_shear(kernel, parts, rows, full_rows, puts, into=None):
    count = len(parts)
    operands = list(parts) + ([] if into is None else [into])
    return pl.pallas_call(
        kernel,
        out_shape=jax.ShapeDtypeStruct((SLAB, ROWS, COLS), jnp.bfloat16),
        in_specs=[HBM] * len(operands),
        out_specs=HBM,
        scratch_shapes=[
            pltpu.VMEM((count, SLAB, BLOCK, COLS), jnp.bfloat16),
            pltpu.VMEM((SLAB, full_rows, COLS), jnp.float32),
            pltpu.VMEM((SLAB, rows, COLS), jnp.bfloat16),
            pltpu.SemaphoreType.DMA((count,)),
            pltpu.SemaphoreType.DMA((SLAB,) + puts),
        ],
        input_output_aliases={} if into is None else {count: 0},
        compiler_params=pltpu.CompilerParams(vmem_limit_bytes=VMEM_LIMIT),
        cost_estimate=COST,
        name="shear_rows",
    )(*operands)


def pairs_of(c):
    found = [(s, s - c) for s in range(SCANS) if 0 <= s - c < SCANS]
    if c < 0:
        found.append((SCANS - 1, -c - 1))
    return found


def local(raw, offsets):
    up = [(i, i + 1) for i in range(SCANS - 1)]
    down = [((i + 1) % SCANS, i) for i in range(SCANS)]
    right = [(i, i + 1) for i in range(3)]
    left = [(i + 1, i) for i in range(3)]
    first, final = halos(offsets, raw)
    after = lax.ppermute(first, "scan", down)
    before = lax.ppermute(final, "scan", up)
    own = pack_edges(raw)
    from_left = lax.ppermute(own, "col", right)
    from_right = lax.ppermute(own, "col", left)
    raw, _ = lax.optimization_barrier((raw, own))
    made = shear(EARLY, offsets, raw, before, after)
    moved = {c: lax.ppermute(part, "scan", pairs_of(c)) for c, part in zip(EARLY, made)}
    lane = lax.broadcasted_iota(jnp.int32, own.shape, 1)
    edges = jnp.where(lane % 32 < 16, from_left, from_right)
    edges, _ = lax.optimization_barrier((edges, made[0]))
    edges_after = lax.ppermute(edges, "scan", down)
    edges_before = lax.ppermute(edges, "scan", up)
    made = shear(LATE, offsets, raw, before, after, column_weights(), edges_before, edges, edges_after)
    parts = dict(zip(LATE, made))
    for c in ORDER[len(EARLY) :]:
        moved[c] = lax.ppermute(parts[c], "scan", pairs_of(c))
    arrived = [moved[c] for c in EARLY]
    own = pack_parts(*arrived)
    arrived = smooth_parts(lax.ppermute(own, "col", right), lax.ppermute(own, "col", left), *arrived)
    moved.update(zip(EARLY, arrived))
    moved[0] = parts[0]
    sooner = ORDER[:-2]
    moved.update(zip(sooner, lax.optimization_barrier([moved[c] for c in sooner])))
    ready = [moved[c] for c in INNER_PARTS]
    result = row_shear(inner_kernel, ready, INNER, (STOP - FIRST) * BLOCK, ())
    rest = [moved[c] for c in OUTER_PARTS]
    full_rows = (FIRST + 1 + SENDS - STOP) * BLOCK + 2 * MARGIN
    return row_shear(outer_kernel, rest, 4 * OUTER, full_rows, (4,), result)


def solution(mesh):
    placed = (P("scan", None, "col"), P("scan"))
    return jax.shard_map(local, mesh=mesh, in_specs=placed, out_specs=P("scan", None, "col"), check_vma=False)
```
